256 devices in a mesh: section: 8 (over z_lo, y), fsdp: 32 (over z_hi, x, core).
Axes of the slice: x: 4, y: 4, z: 8 (z_hi: 4, z_lo: 2; z = z_hi * 2 + z_lo), core: 2. Of those that a mesh axis runs over, the one named last changes fastest.
Arguments:
- hidden: bfloat16 [16384, 7168], P('fsdp', 'section'), may hold values from -600 to 600
- token_ids: int32 [16384], P('fsdp'), may hold values from 0 to 65535
- table: bfloat16 [7168, 65536], P(('section', 'fsdp')), may hold values from -600 to 600
- gain_hidden: float32 [7168], replicated, may hold values from 0.1 to 1.9
- gain_embed: float32 [7168], replicated, may hold values from 0.1 to 1.9
- proj_hidden: bfloat16 [7168, 4096], P(('section', 'fsdp')), may hold values from -0.046875 to 0.046875
- proj_embed: bfloat16 [7168, 4096], P(('section', 'fsdp')), may hold values from -0.046875 to 0.046875
Outputs:
- mixed: bfloat16 [16384, 4096], P('fsdp', 'section')
The draws below stay inside these ranges and needn't reach their ends.
All inputs are finite; a program needn't handle non-finite values.
Results may differ from the reference program's by a relative error of at most 0.0049.
Values may be sent and summed in bfloat16 or wider, within the bound.
No kernel may reach another device: no remote copies, remote signals or barrier semaphores. Data moves between devices by JAX's collectives and lax.ppermute only.
A program may use at most 128 MiB of HBM per device.

```python
import math
import jax
import jax.numpy as jnp
import numpy as np
from jax import lax

D = 7168
DW = 4096
VOCAB = 65536
TOKENS = 16384


def draw_hidden(key, part):
    key = jax.random.fold_in(key, 11)
    first, second, third = jax.random.split(key, 3)
    position = jnp.arange(D, dtype=jnp.float32)[None, :] / (D - 1)
    base = jax.random.normal(first, (TOKENS, D), jnp.float32)
    rows = jnp.exp(jax.random.uniform(second, (TOKENS, 1), jnp.float32) * math.log(10.0))
    rise = jnp.exp(math.log(3.0) * position)
    jitter = jnp.exp(jax.random.uniform(third, (1, D), jnp.float32, -math.log(2.0), math.log(2.0)))
    base = jnp.clip(base, -6.0, 6.0)
    return (base * rows * rise * jitter).astype(jnp.bfloat16)


def draw_table(key, part):
    key = jax.random.fold_in(key, 29)
    first, second, third = jax.random.split(key, 3)
    position = jnp.arange(D, dtype=jnp.float32)[:, None] / (D - 1)
    base = jax.random.normal(first, (D, VOCAB), jnp.float32)
    columns = jnp.exp(jax.random.uniform(second, (1, VOCAB), jnp.float32) * math.log(10.0))
    rise = jnp.exp(math.log(3.0) * position)
    jitter = jnp.exp(jax.random.uniform(third, (D, 1), jnp.float32, -math.log(2.0), math.log(2.0)))
    base = jnp.clip(base, -6.0, 6.0)
    return (base * columns * rise * jitter).astype(jnp.bfloat16)


def place_ends(drawn, own_key, smallest, largest):
    longest = drawn.shape.index(max(drawn.shape))
    spots = []
    for shift in (0, 1):
        where = [jax.random.randint(jax.random.fold_in(own_key, axis), (), 0, length) for axis, length in enumerate(drawn.shape)]
        where[longest] = (where[longest] + shift) % drawn.shape[longest]
        spots.append(tuple(where))
    return drawn.at[spots[0]].set(smallest).at[spots[1]].set(largest)


def levels(own_key, extent, cuts, low, high):
    level, own = 1.0, jax.random.fold_in(own_key, 6)
    for dim, blocks in cuts:
        draws = jnp.exp(jax.random.uniform(jax.random.fold_in(own, dim), (blocks,), jnp.float32, low / len(cuts), high / len(cuts)))
        level = level * jnp.repeat(draws, extent[dim] // blocks).reshape([-1 if axis == dim else 1 for axis in range(len(extent))])
    return level


def rank_table(count, slope):
    loads = [(1 << 20) // math.isqrt(grade ** slope) + 1 for grade in range(1, count + 1)]
    width = 1 + sum(loads) // (1 << 30)
    return np.cumsum(np.array([max(1, weight // width) for weight in loads]))


def ranked_ids(rng, dims, amount, lean):
    listing = rank_table(amount, lean)
    ticket = jax.random.randint(jax.random.fold_in(rng, 1), dims, 0, int(listing[amount - 1]))
    rank = jnp.searchsorted(jnp.asarray(listing, jnp.int32), ticket, side="right")
    return jax.random.permutation(jax.random.fold_in(rng, 2), amount)[rank].astype(jnp.int32)


def normal_values(key, extent, scale, reach, pieces=(), kind=jnp.bfloat16):
    result = jax.random.normal(key, extent, jnp.float32) * scale
    if len(pieces) > 0:
        result = levels(key, extent, pieces, -0.22, 0.18) * result
    return jnp.clip(result, min=-reach, max=reach).astype(kind)


def setup_inputs(seed: int = 0) -> dict:
    splits = jax.random.split(jax.random.key(seed), 8)
    return {
        "hidden": draw_hidden(jax.random.fold_in(splits[7], 71), 0),
        "token_ids": place_ends(ranked_ids(splits[1], (TOKENS,), VOCAB, 2), jax.random.fold_in(splits[1], 3), 0, VOCAB - 1).astype(jnp.int32),
        "table": draw_table(jax.random.fold_in(splits[7], 71), 0),
        "gain_hidden": jnp.clip(1.0 + 0.18 * jax.random.normal(splits[3], (D,), jnp.float32), 0.1, 1.9),
        "gain_embed": jnp.clip(1.0 + 0.18 * jax.random.normal(splits[4], (D,), jnp.float32), 0.1, 1.9),
        "proj_hidden": normal_values(splits[5], (D, DW), (2 * D) ** -0.5, 0.046875, ((0, 256),)),
        "proj_embed": normal_values(splits[6], (D, DW), (2 * D) ** -0.5, 0.046875, ((0, 256),)),
    }


EPS = 1e-06

def normalize(values, gain):
    values_f = values.astype(jnp.float32)
    scale = lax.rsqrt(lax.optimization_barrier(jnp.mean(values_f * values_f, axis=1, keepdims=True)) + EPS)
    return (values_f * scale * gain[None, :]).astype(jnp.bfloat16)

def reference(hidden, token_ids, table, gain_hidden, gain_embed, proj_hidden, proj_embed):
    shifted_ids = jnp.roll(token_ids, -1).astype(jnp.int32)
    embedded = jnp.take(table, shifted_ids, axis=1).T
    hidden_norm = normalize(hidden, gain_hidden)
    embed_norm = normalize(embedded, gain_embed)
    total = jnp.dot(hidden_norm, proj_hidden, preferred_element_type=jnp.float32)
    total = total + jnp.dot(embed_norm, proj_embed, preferred_element_type=jnp.float32)
    return total.astype(jnp.bfloat16)
```

```python
import jax
import jax.numpy as jnp
from jax import lax
from jax.sharding import PartitionSpec as P

EPS = 1e-06
PAD = 32


def on_device(hidden, token_ids, table, gain_hidden, gain_embed, proj_hidden, proj_embed):
    bf, f32 = jnp.bfloat16, jnp.float32
    width = gain_hidden.shape[0]
    tokens, block = hidden.shape
    rows, out_width = proj_hidden.shape
    sections = lax.axis_size("section")
    groups = lax.axis_size("fsdp")
    half = groups // 2
    section = lax.axis_index("section")
    core = lax.axis_index("fsdp") % 2
    same_core = [list(range(c, groups, 2)) for c in range(2)]
    swap = [(i, i ^ 1) for i in range(groups)]

    ids = jnp.roll(lax.all_gather(token_ids, "fsdp", axis=0, tiled=True), -1)

    def panel(w):
        w = jnp.pad(w, ((0, PAD - rows), (0, 0)))
        own = lax.all_gather(w, "fsdp", axis=0, tiled=True, axis_index_groups=same_core)
        return own, lax.ppermute(own, "fsdp", swap)

    wh_own, wh_other = panel(proj_hidden)
    we_own, we_other = panel(proj_embed)

    def across(x):
        total = x
        for d in (1, 2, 4):
            total = total + lax.ppermute(total, "section", [(i, i ^ d) for i in range(sections)])
        return total

    hf = hidden.astype(f32)
    h_scale = lax.rsqrt(across(jnp.sum(hf * hf, axis=1)) / width + EPS)
    gain_h = lax.dynamic_slice_in_dim(gain_hidden, section * block, block)
    hn = (hf * h_scale[:, None] * gain_h[None, :]).astype(bf)
    m = jnp.arange(groups * PAD)
    part, j, r = m // (half * PAD), (m // PAD) % half, m % PAD
    feature = jnp.where(r < rows, (2 * j + (part ^ core)) * rows + r, -1)
    pick = (jnp.arange(block)[:, None] == feature[None, :]).astype(bf)
    hp = jnp.dot(hn, pick, preferred_element_type=f32).astype(bf)
    k = half * PAD
    p_h = jnp.dot(hp[:, :k], wh_own, preferred_element_type=f32) + jnp.dot(
        hp[:, k:], wh_other, preferred_element_type=f32
    )

    looked = jnp.take(table, ids, axis=1, mode="clip")
    looked = jnp.pad(looked, ((0, PAD - rows), (0, 0)))
    e = lax.all_to_all(looked, "fsdp", split_axis=1, concat_axis=0, tiled=True)
    ef = e.astype(f32)
    e_scale = lax.rsqrt(across(jnp.sum(ef * ef, axis=0)) / width + EPS)
    gain_e = lax.dynamic_slice_in_dim(gain_embed, section * block, block).reshape(groups, rows)
    gain_e = jnp.pad(gain_e, ((0, 0), (0, PAD - rows))).reshape(groups * PAD)
    eg = (ef * gain_e[:, None]).astype(bf).reshape(half, 2, PAD, tokens)
    e_own = lax.dynamic_index_in_dim(eg, core, 1, keepdims=False).reshape(k, tokens)
    e_other = lax.dynamic_index_in_dim(eg, 1 - core, 1, keepdims=False).reshape(k, tokens)
    dims = (((0,), (0,)), ((), ()))
    p_e = lax.dot_general(e_own, we_own, dims, preferred_element_type=f32) + lax.dot_general(
        e_other, we_other, dims, preferred_element_type=f32
    )
    part_sum = (p_h + e_scale[:, None] * p_e).astype(bf)
    got = lax.all_to_all(
        part_sum.reshape(tokens, sections, out_width // sections), "section", split_axis=1, concat_axis=1, tiled=True
    )
    return jnp.sum(got.astype(f32), axis=1).astype(bf)


def solution(mesh):
    placed = (
        P("fsdp", "section"),
        P("fsdp"),
        P(("section", "fsdp"), None),
        P(),
        P(),
        P(("section", "fsdp"), None),
        P(("section", "fsdp"), None),
    )
    return jax.shard_map(
        on_device, mesh=mesh, in_specs=placed, out_specs=P("fsdp", "section"), check_vma=False
    )
```

```python
import functools

import jax
import jax.numpy as jnp
from jax import lax
from jax.experimental import pallas as pl
from jax.experimental.pallas import tpu as pltpu
from jax.sharding import PartitionSpec as P

EPS = 1e-06
bf, f32 = jnp.bfloat16, jnp.float32

PAD = 32
LANES = 128
FOLD = LANES // PAD


def turn_kernel(*refs):
    *parts, out = refs
    rows = parts[0].shape[0]
    step = 512
    zero = jnp.zeros((PAD - rows, step), f32)

    def body(i, _):
        at = pl.ds(pl.multiple_of(i * step, step), step)
        stack = []
        for p in parts:
            stack += [p[:, at].astype(f32), zero]
        out[at, :] = jnp.concatenate(stack, axis=0).T
        return 0

    lax.fori_loop(0, out.shape[0] // step, body, 0)


def turn(table, cols=4096):
    rows, vocab = table.shape
    quarter = vocab // FOLD
    per = quarter // cols
    return pl.pallas_call(
        turn_kernel,
        out_shape=jax.ShapeDtypeStruct((quarter, LANES), f32),
        grid=(per,),
        in_specs=[pl.BlockSpec((rows, cols), functools.partial(lambda g, i: (0, g * per + i), g)) for g in range(FOLD)],
        out_specs=pl.BlockSpec((cols, LANES), lambda i: (i, 0)),
        compiler_params=pltpu.CompilerParams(vmem_limit_bytes=60 << 20),
        cost_estimate=pl.CostEstimate(flops=0, bytes_accessed=3 * rows * vocab * 2, transcendentals=0),
        name="turn",
    )(*[table] * FOLD)


def look_kernel(quarter, row_ref, grp_ref, tab_ref, out_ref, g_ref):
    d = pl.program_id(0)
    tokens = out_ref.shape[2]
    for b in range(tokens // LANES):
        base = b * LANES
        for t in range(LANES):
            r = row_ref[d, 0, base + t]
            g_ref[b, pl.ds(t, 1), :] = tab_ref[r]
    for b in range(tokens // LANES):
        base = b * LANES
        turned = g_ref[b].T
        grp = grp_ref[0, :, base : base + LANES]
        val = turned[:PAD]
        for g in range(1, FOLD):
            val = jnp.where(grp == g, turned[g * PAD : (g + 1) * PAD], val)
        out_ref[0, :, base : base + LANES] = val.astype(bf)


def look(table_t, ids):
    quarter = table_t.shape[0]
    dests, tokens = ids.shape
    row = (ids % quarter).reshape(dests, 1, tokens)
    grp = (ids // quarter).reshape(dests, 1, tokens)
    return pl.pallas_call(
        functools.partial(look_kernel, quarter),
        out_shape=jax.ShapeDtypeStruct((dests, PAD, tokens), bf),
        grid=(dests,),
        in_specs=[
            pl.BlockSpec(memory_space=pltpu.SMEM),
            pl.BlockSpec((1, 1, tokens), lambda d: (d, 0, 0)),
            pl.BlockSpec((quarter, 1, LANES), lambda d: (0, 0, 0), pipeline_mode=pl.Buffered(1)),
        ],
        out_specs=pl.BlockSpec((1, PAD, tokens), lambda d: (d, 0, 0)),
        scratch_shapes=[pltpu.VMEM((tokens // LANES, LANES, LANES), f32)],
        compiler_params=pltpu.CompilerParams(vmem_limit_bytes=40 << 20),
        name="look",
    )(row, grp, table_t.reshape(quarter, 1, LANES))


def prep_kernel(h_ref, e_ref, s_ref, out_ref, all_ref):
    groups, pad, tokens = e_ref.shape
    deep = groups * pad
    for i in range(deep // LANES):
        part = e_ref[i * LANES // pad : (i + 1) * LANES // pad].reshape(LANES, tokens)
        all_ref[:, i * LANES : (i + 1) * LANES] = part.astype(f32).T.astype(bf)
    all_ref[:, deep:] = h_ref[...]
    step = 256

    def body(i, _):
        at = pl.ds(pl.multiple_of(i * step, step), step)
        want = s_ref[:, at]
        pick = (lax.broadcasted_iota(jnp.int32, (all_ref.shape[1], step), 0) == want).astype(f32).astype(bf)
        out_ref[:, at] = jnp.dot(all_ref[...], pick, preferred_element_type=f32).astype(bf)
        return 0

    lax.fori_loop(0, out_ref.shape[1] // step, body, 0)


def prep(h, e, source):
    tokens, block = h.shape
    depth = source.shape[1]
    deep = block + e.shape[0] * e.shape[1]
    return pl.pallas_call(
        prep_kernel,
        out_shape=jax.ShapeDtypeStruct((tokens, depth), bf),
        scratch_shapes=[pltpu.VMEM((tokens, deep), bf)],
        compiler_params=pltpu.CompilerParams(vmem_limit_bytes=40 << 20),
        cost_estimate=pl.CostEstimate(flops=2 * tokens * deep * depth, bytes_accessed=8 << 20, transcendentals=0),
        name="prep",
    )(h, e, source)


def mix_kernel(n_pieces, *refs):
    x_ref, g_ref, m_ref, s_ref = refs[:4]
    pieces = refs[4 : 4 + n_pieces]
    out_ref, left_ref = refs[4 + n_pieces :]

    @pl.when(pl.program_id(0) == 0)
    def _():
        tokens, depth = x_ref.shape
        scale_h = jnp.broadcast_to(s_ref[0:1], (LANES, tokens)).T
        scale_e = jnp.broadcast_to(s_ref[1:2], (LANES, tokens)).T
        for i in range(depth // LANES):
            at = slice(i * LANES, (i + 1) * LANES)
            scale = jnp.where(m_ref[:, at] > 0, scale_h, scale_e)
            left_ref[:, at] = (x_ref[:, at].astype(f32) * scale * g_ref[:, at]).astype(bf)

    at, acc = 0, None
    for p in pieces:
        rows = p.shape[0]
        term = jnp.dot(left_ref[:, at : at + rows], p[...], preferred_element_type=f32)
        acc = term if acc is None else acc + term
        at += rows
    out_ref[0] = acc.astype(bf)


def mix(x, gain, is_hidden, scales, pieces, sections):
    tokens, depth = x.shape
    cols = pieces[0].shape[1] // sections
    whole = lambda n: (0, 0)
    return pl.pallas_call(
        functools.partial(mix_kernel, len(pieces)),
        out_shape=jax.ShapeDtypeStruct((sections, tokens, cols), bf),
        grid=(sections,),
        in_specs=[pl.BlockSpec(a.shape, whole) for a in (x, gain, is_hidden, scales)]
        + [pl.BlockSpec((p.shape[0], cols), lambda n: (0, n)) for p in pieces],
        out_specs=pl.BlockSpec((1, tokens, cols), lambda n: (n, 0, 0)),
        scratch_shapes=[pltpu.VMEM((tokens, depth), bf)],
        compiler_params=pltpu.CompilerParams(vmem_limit_bytes=60 << 20),
        cost_estimate=pl.CostEstimate(
            flops=2 * tokens * depth * cols * sections, bytes_accessed=4 * depth * cols * sections, transcendentals=0
        ),
        name="mix",
    )(x, gain, is_hidden, scales, *pieces)


def add_kernel(x_ref, out_ref):
    total = x_ref[0].astype(f32)
    for i in range(1, x_ref.shape[0]):
        total = total + x_ref[i].astype(f32)
    out_ref[...] = total.astype(bf)


def add_parts(x, step=128):
    parts, tokens, cols = x.shape
    return pl.pallas_call(
        add_kernel,
        out_shape=jax.ShapeDtypeStruct((tokens, cols), bf),
        grid=(tokens // step,),
        in_specs=[pl.BlockSpec((parts, step, cols), lambda i: (0, i, 0))],
        out_specs=pl.BlockSpec((step, cols), lambda i: (i, 0)),
        name="add_parts",
    )(x)


def spread(w):
    f = lax.axis_index("fsdp")
    z, x, c = f // 8, (f // 2) % 4, f % 2

    def to(a, dz, dx, dc=0):
        pairs = []
        for i in range(lax.axis_size("fsdp")):
            iz, ix, ic = i // 8, (i // 2) % 4, i % 2
            pairs.append((i, ((iz + dz) % 4) * 8 + ((ix + dx) % 4) * 2 + (ic ^ dc)))
        return lax.ppermute(a, "fsdp", pairs)

    line = jnp.concatenate([w, to(w, 1, 0), to(w, -1, 0), to(w, 2, 0)], axis=0)
    own = jnp.concatenate([line, to(line, 0, 1), to(line, 0, -1), to(line, 0, 2)], axis=0)
    other = to(own, 0, 0, 1)
    home = [
        ((z + dz) % 4) * 8 + ((x + dx) % 4) * 2 + (c ^ dc)
        for dc in range(2)
        for dx in (0, -1, 1, 2)
        for dz in (0, -1, 1, 2)
    ]
    return line, own, other, jnp.stack(home)


HEAD = 40


def on_device(hidden, token_ids, table, gain_hidden, gain_embed, proj_hidden, proj_embed):
    width = gain_hidden.shape[0]
    tokens, block = hidden.shape
    rows, out_width = proj_hidden.shape
    sections = lax.axis_size("section")
    groups = lax.axis_size("fsdp")
    section = lax.axis_index("section")
    cut = HEAD - rows

    ids = lax.all_to_all(
        jnp.broadcast_to(token_ids[None], (groups, tokens)), "fsdp", split_axis=0, concat_axis=0, tiled=True
    )
    main = lax.all_gather(jnp.concatenate([proj_hidden, proj_embed[:cut]], axis=0), "fsdp", axis=0, tiled=True)
    line, own, other, home = spread(proj_embed[cut:])

    f, r = jnp.arange(groups)[:, None], jnp.arange(HEAD)[None, :]
    source = jnp.where(r < rows, groups * PAD + f * rows + r, f * PAD + r - rows)
    tail = home[:, None] * PAD + cut + jnp.arange(rows - cut)[None, :]
    source = jnp.concatenate([source.reshape(-1), tail.reshape(-1)])[None, :]
    is_hidden = (source >= groups * PAD).astype(f32)
    gain_h = lax.dynamic_slice_in_dim(gain_hidden, section * block, block).reshape(groups, rows)
    gain_e = lax.dynamic_slice_in_dim(gain_embed, section * block, block).reshape(groups, rows)
    gain_t = jnp.sum(jnp.where(home[:, None, None] == f[None], gain_e[None, :, cut:], 0.0), axis=1)
    gain = jnp.concatenate(
        [jnp.concatenate([gain_h, gain_e[:, :cut]], axis=1).reshape(-1), gain_t.reshape(-1)]
    )[None, :]
    hf = hidden.astype(f32)
    h_sq = jnp.sum(hf * hf, axis=1)

    turned = turn(table)
    ids, line = lax.optimization_barrier((ids, line))
    ids = jnp.roll(ids.reshape(-1), -1).reshape(groups, tokens)
    looked = look(turned, ids)
    e = lax.all_to_all(looked, "fsdp", split_axis=0, concat_axis=0, tiled=True)
    ef = e.astype(f32)
    squares = jnp.stack([h_sq, jnp.sum(ef * ef, axis=(0, 1))])
    squares = lax.all_to_all(
        jnp.broadcast_to(squares[None], (sections, 2, tokens)), "section", split_axis=0, concat_axis=0, tiled=True
    )
    scales = lax.rsqrt(jnp.sum(squares, axis=0) / width + EPS)
    x = prep(hidden, e, source)
    sums = mix(x, gain, is_hidden, scales, [main, own, other], sections)
    got = lax.all_to_all(sums, "section", split_axis=0, concat_axis=0, tiled=True)
    return add_parts(got)


def solution(mesh):
    placed = (
        P("fsdp", "section"),
        P("fsdp"),
        P(("section", "fsdp"), None),
        P(),
        P(),
        P(("section", "fsdp"), None),
        P(("section", "fsdp"), None),
    )
    return jax.shard_map(
        on_device, mesh=mesh, in_specs=placed, out_specs=P("fsdp", "section"), check_vma=False
    )
```

```python
import functools

import jax
import jax.numpy as jnp
from jax import lax
from jax.experimental import pallas as pl
from jax.experimental.pallas import tpu as pltpu
from jax.sharding import PartitionSpec as P

EPS = 1e-06
bf, f32 = jnp.bfloat16, jnp.float32

PAD = 32
LANES = 128
FOLD = LANES // PAD


def turn_kernel(*refs):
    *parts, out = refs
    rows = parts[0].shape[0]
    step = 512
    zero = jnp.zeros((PAD - rows, step), f32)

    def body(i, _):
        at = pl.ds(pl.multiple_of(i * step, step), step)
        stack = []
        for p in parts:
            stack += [p[:, at].astype(f32), zero]
        out[at, :] = jnp.concatenate(stack, axis=0).T
        return 0

    lax.fori_loop(0, out.shape[0] // step, body, 0)


def turn(table, cols=4096):
    rows, vocab = table.shape
    quarter = vocab // FOLD
    per = quarter // cols
    return pl.pallas_call(
        turn_kernel,
        out_shape=jax.ShapeDtypeStruct((quarter, LANES), f32),
        grid=(per,),
        in_specs=[pl.BlockSpec((rows, cols), functools.partial(lambda g, i: (0, g * per + i), g)) for g in range(FOLD)],
        out_specs=pl.BlockSpec((cols, LANES), lambda i: (i, 0)),
        compiler_params=pltpu.CompilerParams(vmem_limit_bytes=60 << 20),
        name="turn",
    )(*[table] * FOLD)


def look_kernel(quarter, row_ref, grp_ref, tab_ref, out_ref, g_ref):
    d = pl.program_id(0)
    tokens = out_ref.shape[2]
    for b in range(tokens // LANES):
        base = b * LANES
        for t in range(LANES):
            r = row_ref[d, 0, base + t]
            g_ref[b, pl.ds(t, 1), :] = tab_ref[r]
    for b in range(tokens // LANES):
        base = b * LANES
        turned = g_ref[b].T
        grp = grp_ref[0, :, base : base + LANES]
        val = turned[:PAD]
        for g in range(1, FOLD):
            val = jnp.where(grp == g, turned[g * PAD : (g + 1) * PAD], val)
        out_ref[0, :, base : base + LANES] = val.astype(bf)


def look(table_t, ids):
    quarter = table_t.shape[0]
    dests, tokens = ids.shape
    row = (ids % quarter).reshape(dests, 1, tokens)
    grp = (ids // quarter).reshape(dests, 1, tokens)
    return pl.pallas_call(
        functools.partial(look_kernel, quarter),
        out_shape=jax.ShapeDtypeStruct((dests, PAD, tokens), bf),
        grid=(dests,),
        in_specs=[
            pl.BlockSpec(memory_space=pltpu.SMEM),
            pl.BlockSpec((1, 1, tokens), lambda d: (d, 0, 0)),
            pl.BlockSpec((quarter, 1, LANES), lambda d: (0, 0, 0), pipeline_mode=pl.Buffered(1)),
        ],
        out_specs=pl.BlockSpec((1, PAD, tokens), lambda d: (d, 0, 0)),
        scratch_shapes=[pltpu.VMEM((tokens // LANES, LANES, LANES), f32)],
        compiler_params=pltpu.CompilerParams(vmem_limit_bytes=40 << 20),
        name="look",
    )(row, grp, table_t.reshape(quarter, 1, LANES))


def prep_kernel(h_ref, e_ref, s_ref, out_ref, all_ref):
    groups, pad, tokens = e_ref.shape
    deep = groups * pad
    for i in range(deep // LANES):
        part = e_ref[i * LANES // pad : (i + 1) * LANES // pad].reshape(LANES, tokens)
        all_ref[:, i * LANES : (i + 1) * LANES] = part.astype(f32).T.astype(bf)
    all_ref[:, deep:] = h_ref[...]
    step = 256

    def body(i, _):
        at = pl.ds(pl.multiple_of(i * step, step), step)
        want = s_ref[:, at]
        pick = (lax.broadcasted_iota(jnp.int32, (all_ref.shape[1], step), 0) == want).astype(f32).astype(bf)
        out_ref[:, at] = jnp.dot(all_ref[...], pick, preferred_element_type=f32).astype(bf)
        return 0

    lax.fori_loop(0, out_ref.shape[1] // step, body, 0)


def prep(h, e, source):
    tokens, block = h.shape
    depth = source.shape[1]
    deep = block + e.shape[0] * e.shape[1]
    return pl.pallas_call(
        prep_kernel,
        out_shape=jax.ShapeDtypeStruct((tokens, depth), bf),
        scratch_shapes=[pltpu.VMEM((tokens, deep), bf)],
        compiler_params=pltpu.CompilerParams(vmem_limit_bytes=40 << 20),
        cost_estimate=pl.CostEstimate(flops=2 * tokens * deep * depth, bytes_accessed=8 << 20, transcendentals=0),
        name="prep",
    )(h, e, source)


def mix_kernel(n_pieces, order_ref, *refs):
    x_ref, g_ref, m_ref, s_ref = refs[:4]
    pieces = refs[4 : 4 + n_pieces]
    a_send, a_keep, b_1, b_2, b_3, b_keep, left_ref = refs[4 + n_pieces :]
    n = pl.program_id(0)
    side = n % 4

    @pl.when(n == 0)
    def _():
        tokens, depth = x_ref.shape
        scale_h = jnp.broadcast_to(s_ref[0:1], (LANES, tokens)).T
        scale_e = jnp.broadcast_to(s_ref[1:2], (LANES, tokens)).T
        for i in range(depth // LANES):
            at = slice(i * LANES, (i + 1) * LANES)
            scale = jnp.where(m_ref[:, at] > 0, scale_h, scale_e)
            left_ref[:, at] = (x_ref[:, at].astype(f32) * scale * g_ref[:, at]).astype(bf)

    at, acc = 0, None
    for p in pieces:
        rows = p.shape[0]
        term = jnp.dot(left_ref[:, at : at + rows], p[...], preferred_element_type=f32)
        acc = term if acc is None else acc + term
        at += rows
    half = acc.shape[1] // 2

    @pl.when(n < 4)
    def _():
        a_send[0] = acc[:, :half].astype(bf)

    @pl.when(n >= 4)
    def _():
        a_keep[0] = acc[:, :half]

    for i, ref in enumerate((b_1, b_2, b_3, b_keep)):

        @pl.when(side == i)
        def _():
            ref[0] = acc[:, half:].astype(ref.dtype)


def mix(x, gain, is_hidden, scales, pieces, sections):
    tokens, depth = x.shape
    cols = pieces[0].shape[1] // sections
    half = cols // 2
    section = lax.axis_index("section")
    z, y = section // 4, section % 4
    order = jnp.stack([(zz * 4 + (y + 1 + i) % 4) for zz in (1 - z, z) for i in range(4)])
    whole = lambda n, order: (0, 0)
    block = lambda place: pl.BlockSpec((1, tokens, half), lambda n, order: (place(n), 0, 0))
    shape = lambda count, kind: jax.ShapeDtypeStruct((count, tokens, half), kind)
    later = lambda i: lambda n: jnp.where(n < 4 + i, 0, 1)
    return pl.pallas_call(
        functools.partial(mix_kernel, len(pieces)),
        out_shape=[shape(4, bf), shape(4, f32), shape(2, bf), shape(2, bf), shape(2, bf), shape(2, f32)],
        grid_spec=pltpu.PrefetchScalarGridSpec(
            num_scalar_prefetch=1,
            grid=(sections,),
            in_specs=[pl.BlockSpec(a.shape, whole) for a in (x, gain, is_hidden, scales)]
            + [pl.BlockSpec((p.shape[0], cols), lambda n, order: (0, order[n])) for p in pieces],
            out_specs=[block(lambda n: jnp.minimum(n, 3)), block(lambda n: jnp.maximum(n - 4, 0))]
            + [block(later(i)) for i in range(4)],
            scratch_shapes=[pltpu.VMEM((tokens, depth), bf)],
        ),
        compiler_params=pltpu.CompilerParams(vmem_limit_bytes=50 << 20),
        cost_estimate=pl.CostEstimate(
            flops=2 * tokens * depth * cols * sections, bytes_accessed=4 * depth * cols * sections, transcendentals=0
        ),
        name="mix",
    )(order, x, gain, is_hidden, scales, *pieces)


def fold_kernel(a_keep, a_in, b_keep, b_1, b_2, b_3, a_1, a_2, a_3, a_own, b_send, b_own):
    for i, ref in enumerate((a_1, a_2, a_3, a_own)):
        ref[...] = (a_keep[i] + a_in[i].astype(f32)).astype(ref.dtype)
    for i, ref in enumerate((b_send, b_own)):
        total = b_keep[i] + b_1[i].astype(f32) + b_2[i].astype(f32) + b_3[i].astype(f32)
        ref[...] = total.astype(ref.dtype)


def last_kernel(a_own, a_1, a_2, a_3, b_own, b_in, out_ref):
    half = a_own.shape[1]
    out_ref[:, :half] = (a_own[...] + a_1[...].astype(f32) + a_2[...].astype(f32) + a_3[...].astype(f32)).astype(bf)
    out_ref[:, half:] = (b_own[...] + b_in[...].astype(f32)).astype(bf)


def fold(a_send, a_keep, b_1, b_2, b_3, b_keep, step=128):
    count = lax.axis_size("section")
    _, tokens, half = a_keep.shape

    def to(a, dz, dy):
        pairs = [(i, ((i // 4 + dz) % 2) * 4 + (i % 4 + dy) % 4) for i in range(count)]
        return lax.ppermute(a, "section", pairs)

    b_in = [to(b, 0, d) for b, d in ((b_1, 1), (b_2, 2), (b_3, 3))]
    a_in = to(a_send, 1, 0)
    deep = lambda n: pl.BlockSpec((n, step, half), lambda i: (0, i, 0))
    flat = pl.BlockSpec((step, half), lambda i: (i, 0))
    shape = lambda kind: jax.ShapeDtypeStruct((tokens, half), kind)
    a_1, a_2, a_3, a_own, b_send, b_own = pl.pallas_call(
        fold_kernel,
        out_shape=[shape(bf)] * 3 + [shape(f32), shape(bf), shape(f32)],
        grid=(tokens // step,),
        in_specs=[deep(4), deep(4), deep(2), deep(2), deep(2), deep(2)],
        out_specs=[flat] * 6,
        compiler_params=pltpu.CompilerParams(vmem_limit_bytes=16 << 20),
        name="fold",
    )(a_keep, a_in, b_keep, *b_in)
    a_more = [to(a, 0, d) for a, d in ((a_1, 1), (a_2, 2), (a_3, 3))]
    b_more = to(b_send, 1, 0)
    return pl.pallas_call(
        last_kernel,
        out_shape=jax.ShapeDtypeStruct((tokens, 2 * half), bf),
        grid=(tokens // step,),
        in_specs=[flat] * 6,
        out_specs=pl.BlockSpec((step, 2 * half), lambda i: (i, 0)),
        compiler_params=pltpu.CompilerParams(vmem_limit_bytes=16 << 20),
        name="last",
    )(a_own, *a_more, b_own, b_more)


def spread(w):
    f = lax.axis_index("fsdp")
    z, x, c = f // 8, (f // 2) % 4, f % 2

    def to(a, dz, dx, dc=0):
        pairs = []
        for i in range(lax.axis_size("fsdp")):
            iz, ix, ic = i // 8, (i // 2) % 4, i % 2
            pairs.append((i, ((iz + dz) % 4) * 8 + ((ix + dx) % 4) * 2 + (ic ^ dc)))
        return lax.ppermute(a, "fsdp", pairs)

    line = jnp.concatenate([w, to(w, 1, 0), to(w, -1, 0), to(w, 2, 0)], axis=0)
    own = jnp.concatenate([line, to(line, 0, 1), to(line, 0, -1), to(line, 0, 2)], axis=0)
    pieces = [own, to(own, 0, 0, 1)]
    home = [
        ((z + dz) % 4) * 8 + ((x + dx) % 4) * 2 + (c ^ dc)
        for dc in range(2)
        for dx in (0, -1, 1, 2)
        for dz in (0, -1, 1, 2)
    ]
    return line, pieces, jnp.stack(home)


HEAD = 40


def on_device(hidden, token_ids, table, gain_hidden, gain_embed, proj_hidden, proj_embed):
    width = gain_hidden.shape[0]
    tokens, block = hidden.shape
    rows, out_width = proj_hidden.shape
    sections = lax.axis_size("section")
    groups = lax.axis_size("fsdp")
    section = lax.axis_index("section")
    both = jnp.concatenate([proj_hidden, proj_embed], axis=0)
    depth = 2 * rows

    ids = lax.all_to_all(
        jnp.broadcast_to(token_ids[None], (groups, tokens)), "fsdp", split_axis=0, concat_axis=0, tiled=True
    )
    main = lax.all_gather(both[:HEAD], "fsdp", axis=0, tiled=True)

    turned = turn(table)
    ids = jnp.roll(ids.reshape(-1), -1).reshape(groups, tokens)
    looked = look(turned, ids)
    tail_rows = both[HEAD:]
    e = lax.all_to_all(looked, "fsdp", split_axis=0, concat_axis=0, tiled=True)
    line, pieces, home = spread(tail_rows)

    f, r = jnp.arange(groups)[:, None], jnp.arange(depth)[None, :]

    def place(f, r):
        return jnp.where(r < rows, groups * PAD + f * rows + r, f * PAD + r - rows).reshape(-1)

    source = jnp.concatenate([place(f, r[:, :HEAD]), place(home[:, None], r[:, HEAD:])])[None, :]
    is_hidden = (source >= groups * PAD).astype(f32)
    gain_h = lax.dynamic_slice_in_dim(gain_hidden, section * block, block).reshape(groups, rows)
    gain_e = lax.dynamic_slice_in_dim(gain_embed, section * block, block).reshape(groups, rows)
    gains = jnp.concatenate([gain_h, gain_e], axis=1)
    gain_t = jnp.sum(jnp.where(home[:, None, None] == f[None], gains[None, :, HEAD:], 0.0), axis=1)
    gain = jnp.concatenate([gains[:, :HEAD].reshape(-1), gain_t.reshape(-1)])[None, :]
    hf = hidden.astype(f32)
    ef = e.astype(f32)
    squares = jnp.stack([jnp.sum(hf * hf, axis=1), jnp.sum(ef * ef, axis=(0, 1))])
    squares = lax.all_to_all(
        jnp.broadcast_to(squares[None], (sections, 2, tokens)), "section", split_axis=0, concat_axis=0, tiled=True
    )
    scales = lax.rsqrt(jnp.sum(squares, axis=0) / width + EPS)
    x = prep(hidden, e, source)
    return fold(*mix(x, gain, is_hidden, scales, [main] + pieces, sections))


def solution(mesh):
    placed = (
        P("fsdp", "section"),
        P("fsdp"),
        P(("section", "fsdp"), None),
        P(),
        P(),
        P(("section", "fsdp"), None),
        P(("section", "fsdp"), None),
    )
    return jax.shard_map(
        on_device, mesh=mesh, in_specs=placed, out_specs=P("fsdp", "section"), check_vma=False
    )
```

```python
import functools

import jax
import jax.numpy as jnp
from jax import lax
from jax.experimental import pallas as pl
from jax.experimental.pallas import tpu as pltpu
from jax.sharding import PartitionSpec as P

EPS = 1e-06
bf, f32 = jnp.bfloat16, jnp.float32

PAD = 32
LANES = 128
FOLD = LANES // PAD


def turn_kernel(*refs):
    *parts, out = refs
    rows = parts[0].shape[0]
    step = 512
    zero = jnp.zeros((PAD - rows, step), f32)

    def body(i, _):
        at = pl.ds(pl.multiple_of(i * step, step), step)
        stack = []
        for p in parts:
            stack += [p[:, at].astype(f32), zero]
        out[at, :] = jnp.concatenate(stack, axis=0).T
        return 0

    lax.fori_loop(0, out.shape[0] // step, body, 0)


def turn(table, cols=4096):
    rows, vocab = table.shape
    quarter = vocab // FOLD
    per = quarter // cols
    return pl.pallas_call(
        turn_kernel,
        out_shape=jax.ShapeDtypeStruct((quarter, LANES), f32),
        grid=(per,),
        in_specs=[pl.BlockSpec((rows, cols), functools.partial(lambda g, i: (0, g * per + i), g)) for g in range(FOLD)],
        out_specs=pl.BlockSpec((cols, LANES), lambda i: (i, 0)),
        compiler_params=pltpu.CompilerParams(vmem_limit_bytes=60 << 20),
        name="turn",
    )(*[table] * FOLD)


def look_kernel(quarter, row_ref, grp_ref, tab_ref, out_ref, g_ref):
    d = pl.program_id(0)
    tokens = out_ref.shape[2]
    for b in range(tokens // LANES):
        base = b * LANES
        for t in range(LANES):
            r = row_ref[d, 0, base + t]
            g_ref[b, pl.ds(t, 1), :] = tab_ref[r]
    for b in range(tokens // LANES):
        base = b * LANES
        turned = g_ref[b].T
        grp = grp_ref[0, :, base : base + LANES]
        val = turned[:PAD]
        for g in range(1, FOLD):
            val = jnp.where(grp == g, turned[g * PAD : (g + 1) * PAD], val)
        out_ref[0, :, base : base + LANES] = val.astype(bf)


def look(table_t, ids):
    quarter = table_t.shape[0]
    dests, tokens = ids.shape
    row = (ids % quarter).reshape(dests, 1, tokens)
    grp = (ids // quarter).reshape(dests, 1, tokens)
    return pl.pallas_call(
        functools.partial(look_kernel, quarter),
        out_shape=jax.ShapeDtypeStruct((dests, PAD, tokens), bf),
        grid=(dests,),
        in_specs=[
            pl.BlockSpec(memory_space=pltpu.SMEM),
            pl.BlockSpec((1, 1, tokens), lambda d: (d, 0, 0)),
            pl.BlockSpec((quarter, 1, LANES), lambda d: (0, 0, 0), pipeline_mode=pl.Buffered(1)),
        ],
        out_specs=pl.BlockSpec((1, PAD, tokens), lambda d: (d, 0, 0)),
        scratch_shapes=[pltpu.VMEM((tokens // LANES, LANES, LANES), f32)],
        compiler_params=pltpu.CompilerParams(vmem_limit_bytes=40 << 20),
        name="look",
    )(row, grp, table_t.reshape(quarter, 1, LANES))


def prep_kernel(h_ref, e_ref, s_ref, out_ref, all_ref):
    groups, pad, tokens = e_ref.shape
    deep = groups * pad
    for i in range(deep // LANES):
        part = e_ref[i * LANES // pad : (i + 1) * LANES // pad].reshape(LANES, tokens)
        all_ref[:, i * LANES : (i + 1) * LANES] = part.astype(f32).T.astype(bf)
    all_ref[:, deep:] = h_ref[...]
    step = 256

    def body(i, _):
        at = pl.ds(pl.multiple_of(i * step, step), step)
        want = s_ref[:, at]
        pick = (lax.broadcasted_iota(jnp.int32, (all_ref.shape[1], step), 0) == want).astype(f32).astype(bf)
        out_ref[:, at] = jnp.dot(all_ref[...], pick, preferred_element_type=f32).astype(bf)
        return 0

    lax.fori_loop(0, out_ref.shape[1] // step, body, 0)


def prep(h, e, source):
    tokens, block = h.shape
    depth = source.shape[1]
    deep = block + e.shape[0] * e.shape[1]
    return pl.pallas_call(
        prep_kernel,
        out_shape=jax.ShapeDtypeStruct((tokens, depth), bf),
        scratch_shapes=[pltpu.VMEM((tokens, deep), bf)],
        compiler_params=pltpu.CompilerParams(vmem_limit_bytes=40 << 20),
        cost_estimate=pl.CostEstimate(flops=2 * tokens * deep * depth, bytes_accessed=8 << 20, transcendentals=0),
        name="prep",
    )(h, e, source)


def product(left_ref, pieces):
    at, acc = 0, None
    for p in pieces:
        rows = p.shape[0]
        term = jnp.dot(left_ref[:, at : at + rows], p[...], preferred_element_type=f32)
        acc = term if acc is None else acc + term
        at += rows
    return acc


def send_kernel(n_pieces, order_ref, *refs):
    x_ref, g_ref, m_ref, s_ref = refs[:4]
    pieces = refs[4 : 4 + n_pieces]
    a_send, b_1, b_2, b_3, left_ref = refs[4 + n_pieces :]
    n = pl.program_id(0)

    @pl.when(n == 0)
    def _():
        tokens, depth = x_ref.shape
        scale_h = jnp.broadcast_to(s_ref[0:1], (LANES, tokens)).T
        scale_e = jnp.broadcast_to(s_ref[1:2], (LANES, tokens)).T
        for i in range(depth // LANES):
            at = slice(i * LANES, (i + 1) * LANES)
            scale = jnp.where(m_ref[:, at] > 0, scale_h, scale_e)
            left_ref[:, at] = (x_ref[:, at].astype(f32) * scale * g_ref[:, at]).astype(bf)

    value = product(left_ref, pieces).astype(bf)
    for ref, first, end in ((a_send, 0, 4), (b_1, 4, 6), (b_2, 6, 8), (b_3, 8, 10)):

        @pl.when((n >= first) & (n < end))
        def _():
            ref[0] = value


def keep_kernel(n_pieces, order_ref, left_ref, *refs):
    pieces = refs[:n_pieces]
    a_keep, b_keep = refs[n_pieces:]
    n = pl.program_id(0)
    value = product(left_ref, pieces)

    @pl.when(n < 4)
    def _():
        a_keep[0] = value

    @pl.when(n >= 4)
    def _():
        b_keep[0] = value


def mix(x, gain, is_hidden, scales, pieces, sections):
    tokens, depth = x.shape
    half = pieces[0].shape[1] // sections // 2
    section = lax.axis_index("section")
    z, y = section // 4, section % 4
    place = lambda zz, d, part: (zz * 4 + (y + d) % 4) * 2 + part
    out_order = [place(1 - z, d, 0) for d in (1, 2, 3, 0)] + [place(zz, d, 1) for d in (1, 2, 3) for zz in (1 - z, z)]
    own_order = [place(z, d, 0) for d in (1, 2, 3, 0)] + [place(zz, 0, 1) for zz in (1 - z, z)]
    whole = lambda n, order: (0, 0)
    columns = [pl.BlockSpec((p.shape[0], half), lambda n, order: (0, order[n])) for p in pieces]
    block = lambda first, count: pl.BlockSpec((1, tokens, half), lambda n, order: (jnp.clip(n - first, 0, count - 1), 0, 0))
    shape = lambda count, kind: jax.ShapeDtypeStruct((count, tokens, half), kind)
    params = pltpu.CompilerParams(vmem_limit_bytes=50 << 20)
    cost = lambda steps: pl.CostEstimate(
        flops=2 * tokens * depth * half * steps, bytes_accessed=4 * depth * half * steps, transcendentals=0
    )
    a_send, b_1, b_2, b_3, left = pl.pallas_call(
        functools.partial(send_kernel, len(pieces)),
        out_shape=[shape(4, bf), shape(2, bf), shape(2, bf), shape(2, bf), jax.ShapeDtypeStruct((tokens, depth), bf)],
        grid_spec=pltpu.PrefetchScalarGridSpec(
            num_scalar_prefetch=1,
            grid=(len(out_order),),
            in_specs=[pl.BlockSpec(v.shape, whole) for v in (x, gain, is_hidden, scales)] + columns,
            out_specs=[block(0, 4), block(4, 2), block(6, 2), block(8, 2), pl.BlockSpec((tokens, depth), whole)],
        ),
        compiler_params=params,
        cost_estimate=cost(len(out_order)),
        name="mix_sent",
    )(jnp.stack(out_order), x, gain, is_hidden, scales, *pieces)
    a_keep, b_keep = pl.pallas_call(
        functools.partial(keep_kernel, len(pieces)),
        out_shape=[shape(4, f32), shape(2, f32)],
        grid_spec=pltpu.PrefetchScalarGridSpec(
            num_scalar_prefetch=1,
            grid=(len(own_order),),
            in_specs=[pl.BlockSpec((tokens, depth), whole)] + columns,
            out_specs=[block(0, 4), block(4, 2)],
        ),
        compiler_params=params,
        cost_estimate=cost(len(own_order)),
        name="mix_kept",
    )(jnp.stack(own_order), left, *pieces)
    return a_send, a_keep, b_1, b_2, b_3, b_keep


def fold_kernel(a_keep, a_in, b_keep, b_1, b_2, b_3, a_1, a_2, a_3, a_own, b_send, b_own):
    for i, ref in enumerate((a_1, a_2, a_3, a_own)):
        ref[...] = (a_keep[i] + a_in[i].astype(f32)).astype(ref.dtype)
    for i, ref in enumerate((b_send, b_own)):
        total = b_keep[i] + b_1[i].astype(f32) + b_2[i].astype(f32) + b_3[i].astype(f32)
        ref[...] = total.astype(ref.dtype)


def last_kernel(a_own, a_1, a_2, a_3, b_own, b_in, out_ref):
    half = a_own.shape[1]
    out_ref[:, :half] = (a_own[...] + a_1[...].astype(f32) + a_2[...].astype(f32) + a_3[...].astype(f32)).astype(bf)
    out_ref[:, half:] = (b_own[...] + b_in[...].astype(f32)).astype(bf)


def fold(a_send, a_keep, b_1, b_2, b_3, b_keep, step=128):
    count = lax.axis_size("section")
    _, tokens, half = a_keep.shape

    def to(a, dz, dy):
        pairs = [(i, ((i // 4 + dz) % 2) * 4 + (i % 4 + dy) % 4) for i in range(count)]
        return lax.ppermute(a, "section", pairs)

    b_in = [to(b, 0, d) for b, d in ((b_1, 1), (b_2, 2), (b_3, 3))]
    a_in = to(a_send, 1, 0)
    deep = lambda n: pl.BlockSpec((n, step, half), lambda i: (0, i, 0))
    flat = pl.BlockSpec((step, half), lambda i: (i, 0))
    shape = lambda kind: jax.ShapeDtypeStruct((tokens, half), kind)
    a_1, a_2, a_3, a_own, b_send, b_own = pl.pallas_call(
        fold_kernel,
        out_shape=[shape(bf)] * 3 + [shape(f32), shape(bf), shape(f32)],
        grid=(tokens // step,),
        in_specs=[deep(4), deep(4), deep(2), deep(2), deep(2), deep(2)],
        out_specs=[flat] * 6,
        compiler_params=pltpu.CompilerParams(vmem_limit_bytes=16 << 20),
        name="fold",
    )(a_keep, a_in, b_keep, *b_in)
    a_more = [to(a, 0, d) for a, d in ((a_1, 1), (a_2, 2), (a_3, 3))]
    b_more = to(b_send, 1, 0)
    return pl.pallas_call(
        last_kernel,
        out_shape=jax.ShapeDtypeStruct((tokens, 2 * half), bf),
        grid=(tokens // step,),
        in_specs=[flat] * 6,
        out_specs=pl.BlockSpec((step, 2 * half), lambda i: (i, 0)),
        compiler_params=pltpu.CompilerParams(vmem_limit_bytes=16 << 20),
        name="last",
    )(a_own, *a_more, b_own, b_more)


def spread(w):
    f = lax.axis_index("fsdp")
    z, x, c = f // 8, (f // 2) % 4, f % 2

    def to(a, dz, dx, dc=0):
        pairs = []
        for i in range(lax.axis_size("fsdp")):
            iz, ix, ic = i // 8, (i // 2) % 4, i % 2
            pairs.append((i, ((iz + dz) % 4) * 8 + ((ix + dx) % 4) * 2 + (ic ^ dc)))
        return lax.ppermute(a, "fsdp", pairs)

    line = jnp.concatenate([w, to(w, 1, 0), to(w, -1, 0), to(w, 2, 0)], axis=0)
    own = jnp.concatenate([line, to(line, 0, 1), to(line, 0, -1), to(line, 0, 2)], axis=0)
    pieces = [own, to(own, 0, 0, 1)]
    home = [
        ((z + dz) % 4) * 8 + ((x + dx) % 4) * 2 + (c ^ dc)
        for dc in range(2)
        for dx in (0, -1, 1, 2)
        for dz in (0, -1, 1, 2)
    ]
    return line, pieces, jnp.stack(home)


HEAD = 40


def on_device(hidden, token_ids, table, gain_hidden, gain_embed, proj_hidden, proj_embed):
    width = gain_hidden.shape[0]
    tokens, block = hidden.shape
    rows, out_width = proj_hidden.shape
    sections = lax.axis_size("section")
    groups = lax.axis_size("fsdp")
    section = lax.axis_index("section")
    both = jnp.concatenate([proj_hidden, proj_embed], axis=0)
    depth = 2 * rows

    ids = lax.all_to_all(
        jnp.broadcast_to(token_ids[None], (groups, tokens)), "fsdp", split_axis=0, concat_axis=0, tiled=True
    )
    main = lax.all_gather(both[:HEAD], "fsdp", axis=0, tiled=True)

    turned = turn(table)
    ids = jnp.roll(ids.reshape(-1), -1).reshape(groups, tokens)
    looked = look(turned, ids)
    tail_rows = both[HEAD:]
    e = lax.all_to_all(looked, "fsdp", split_axis=0, concat_axis=0, tiled=True)
    line, pieces, home = spread(tail_rows)

    f, r = jnp.arange(groups)[:, None], jnp.arange(depth)[None, :]

    def place(f, r):
        return jnp.where(r < rows, groups * PAD + f * rows + r, f * PAD + r - rows).reshape(-1)

    source = jnp.concatenate([place(f, r[:, :HEAD]), place(home[:, None], r[:, HEAD:])])[None, :]
    is_hidden = (source >= groups * PAD).astype(f32)
    gain_h = lax.dynamic_slice_in_dim(gain_hidden, section * block, block).reshape(groups, rows)
    gain_e = lax.dynamic_slice_in_dim(gain_embed, section * block, block).reshape(groups, rows)
    gains = jnp.concatenate([gain_h, gain_e], axis=1)
    gain_t = jnp.sum(jnp.where(home[:, None, None] == f[None], gains[None, :, HEAD:], 0.0), axis=1)
    gain = jnp.concatenate([gains[:, :HEAD].reshape(-1), gain_t.reshape(-1)])[None, :]
    hf = hidden.astype(f32)
    ef = e.astype(f32)
    squares = jnp.stack([jnp.sum(hf * hf, axis=1), jnp.sum(ef * ef, axis=(0, 1))])
    squares = lax.all_to_all(
        jnp.broadcast_to(squares[None], (sections, 2, tokens)), "section", split_axis=0, concat_axis=0, tiled=True
    )
    scales = lax.rsqrt(jnp.sum(squares, axis=0) / width + EPS)
    x = prep(hidden, e, source)
    return fold(*mix(x, gain, is_hidden, scales, [main] + pieces, sections))


def solution(mesh):
    placed = (
        P("fsdp", "section"),
        P("fsdp"),
        P(("section", "fsdp"), None),
        P(),
        P(),
        P(("section", "fsdp"), None),
        P(("section", "fsdp"), None),
    )
    return jax.shard_map(
        on_device, mesh=mesh, in_specs=placed, out_specs=P("fsdp", "section"), check_vma=False
    )
```

```python
import functools

import jax
import jax.numpy as jnp
from jax import lax
from jax.experimental import pallas as pl
from jax.experimental.pallas import tpu as pltpu
from jax.sharding import PartitionSpec as P

EPS = 1e-06
bf, f32 = jnp.bfloat16, jnp.float32

PAD = 32
LANES = 128
FOLD = LANES // PAD


def turn_kernel(*refs):
    *parts, out = refs
    rows = parts[0].shape[0]
    step = 512
    zero = jnp.zeros((PAD - rows, step), f32)

    def body(i, _):
        at = pl.ds(pl.multiple_of(i * step, step), step)
        stack = []
        for p in parts:
            stack += [p[:, at].astype(f32), zero]
        out[at, :] = jnp.concatenate(stack, axis=0).T
        return 0

    lax.fori_loop(0, out.shape[0] // step, body, 0)


def turn(table, cols=4096):
    rows, vocab = table.shape
    quarter = vocab // FOLD
    per = quarter // cols
    return pl.pallas_call(
        turn_kernel,
        out_shape=jax.ShapeDtypeStruct((quarter, LANES), f32),
        grid=(per,),
        in_specs=[pl.BlockSpec((rows, cols), functools.partial(lambda g, i: (0, g * per + i), g)) for g in range(FOLD)],
        out_specs=pl.BlockSpec((cols, LANES), lambda i: (i, 0)),
        compiler_params=pltpu.CompilerParams(vmem_limit_bytes=60 << 20),
        name="turn",
    )(*[table] * FOLD)


def look_kernel(quarter, row_ref, grp_ref, tab_ref, out_ref, g_ref):
    d = pl.program_id(0)
    tokens = out_ref.shape[2]
    for b in range(tokens // LANES):
        base = b * LANES
        for t in range(LANES):
            r = row_ref[d, 0, base + t]
            g_ref[b, pl.ds(t, 1), :] = tab_ref[r]
    for b in range(tokens // LANES):
        base = b * LANES
        turned = g_ref[b].T
        grp = grp_ref[0, :, base : base + LANES]
        val = turned[:PAD]
        for g in range(1, FOLD):
            val = jnp.where(grp == g, turned[g * PAD : (g + 1) * PAD], val)
        out_ref[0, :, base : base + LANES] = val.astype(bf)


def look(table_t, ids):
    quarter = table_t.shape[0]
    dests, tokens = ids.shape
    row = (ids % quarter).reshape(dests, 1, tokens)
    grp = (ids // quarter).reshape(dests, 1, tokens)
    return pl.pallas_call(
        functools.partial(look_kernel, quarter),
        out_shape=jax.ShapeDtypeStruct((dests, PAD, tokens), bf),
        grid=(dests,),
        in_specs=[
            pl.BlockSpec(memory_space=pltpu.SMEM),
            pl.BlockSpec((1, 1, tokens), lambda d: (d, 0, 0)),
            pl.BlockSpec((quarter, 1, LANES), lambda d: (0, 0, 0), pipeline_mode=pl.Buffered(1)),
        ],
        out_specs=pl.BlockSpec((1, PAD, tokens), lambda d: (d, 0, 0)),
        scratch_shapes=[pltpu.VMEM((tokens // LANES, LANES, LANES), f32)],
        compiler_params=pltpu.CompilerParams(vmem_limit_bytes=40 << 20),
        name="look",
    )(row, grp, table_t.reshape(quarter, 1, LANES))


def prep_kernel(h_ref, e_ref, s_ref, out_ref, all_ref):
    groups, pad, tokens = e_ref.shape
    deep = groups * pad
    for i in range(deep // LANES):
        part = e_ref[i * LANES // pad : (i + 1) * LANES // pad].reshape(LANES, tokens)
        all_ref[:, i * LANES : (i + 1) * LANES] = part.astype(f32).T.astype(bf)
    all_ref[:, deep:] = h_ref[...]
    step = 256

    def body(i, _):
        at = pl.ds(pl.multiple_of(i * step, step), step)
        want = s_ref[:, at]
        pick = (lax.broadcasted_iota(jnp.int32, (all_ref.shape[1], step), 0) == want).astype(f32).astype(bf)
        out_ref[:, at] = jnp.dot(all_ref[...], pick, preferred_element_type=f32).astype(bf)
        return 0

    lax.fori_loop(0, out_ref.shape[1] // step, body, 0)


def prep(h, e, source):
    tokens, block = h.shape
    depth = source.shape[1]
    deep = block + e.shape[0] * e.shape[1]
    return pl.pallas_call(
        prep_kernel,
        out_shape=jax.ShapeDtypeStruct((tokens, depth), bf),
        scratch_shapes=[pltpu.VMEM((tokens, deep), bf)],
        compiler_params=pltpu.CompilerParams(vmem_limit_bytes=40 << 20),
        cost_estimate=pl.CostEstimate(flops=2 * tokens * deep * depth, bytes_accessed=8 << 20, transcendentals=0),
        name="prep",
    )(h, e, source)


def product(left_ref, pieces):
    at, acc = 0, None
    for p in pieces:
        rows = p.shape[0]
        term = jnp.dot(left_ref[:, at : at + rows], p[...], preferred_element_type=f32)
        acc = term if acc is None else acc + term
        at += rows
    return acc


def send_kernel(n_pieces, order_ref, *refs):
    x_ref, g_ref, m_ref, s_ref = refs[:4]
    pieces = refs[4 : 4 + n_pieces]
    a_send, b_1, b_2, b_3, left_ref = refs[4 + n_pieces :]
    n = pl.program_id(0)

    @pl.when(n == 0)
    def _():
        tokens, depth = x_ref.shape
        scale_h = jnp.broadcast_to(s_ref[0:1], (LANES, tokens)).T
        scale_e = jnp.broadcast_to(s_ref[1:2], (LANES, tokens)).T
        for i in range(depth // LANES):
            at = slice(i * LANES, (i + 1) * LANES)
            scale = jnp.where(m_ref[:, at] > 0, scale_h, scale_e)
            left_ref[:, at] = (x_ref[:, at].astype(f32) * scale * g_ref[:, at]).astype(bf)

    value = product(left_ref, pieces).astype(bf)
    for ref, first, end in ((a_send, 0, 4), (b_1, 4, 6), (b_2, 6, 8), (b_3, 8, 10)):

        @pl.when((n >= first) & (n < end))
        def _():
            ref[0] = value


def keep_kernel(n_pieces, order_ref, left_ref, *refs):
    pieces = refs[:n_pieces]
    a_keep, b_keep = refs[n_pieces:]
    n = pl.program_id(0)
    value = product(left_ref, pieces)

    @pl.when(n < 4)
    def _():
        a_keep[0] = value

    @pl.when(n >= 4)
    def _():
        b_keep[0] = value


def mix(x, gain, is_hidden, scales, pieces, sections):
    tokens, depth = x.shape
    half = pieces[0].shape[1] // sections // 2
    section = lax.axis_index("section")
    z, y = section // 4, section % 4
    place = lambda zz, d, part: (zz * 4 + (y + d) % 4) * 2 + part
    out_order = [place(1 - z, d, 0) for d in (1, 2, 3, 0)] + [place(zz, d, 1) for d in (1, 2, 3) for zz in (1 - z, z)]
    own_order = [place(z, d, 0) for d in (1, 2, 3, 0)] + [place(zz, 0, 1) for zz in (1 - z, z)]
    whole = lambda n, order: (0, 0)
    columns = [pl.BlockSpec((p.shape[0], half), lambda n, order: (0, order[n])) for p in pieces]
    block = lambda first, count: pl.BlockSpec((1, tokens, half), lambda n, order: (jnp.clip(n - first, 0, count - 1), 0, 0))
    shape = lambda count, kind: jax.ShapeDtypeStruct((count, tokens, half), kind)
    params = pltpu.CompilerParams(vmem_limit_bytes=50 << 20)
    cost = lambda steps: pl.CostEstimate(
        flops=2 * tokens * depth * half * steps, bytes_accessed=4 * depth * half * steps, transcendentals=0
    )
    a_send, b_1, b_2, b_3, left = pl.pallas_call(
        functools.partial(send_kernel, len(pieces)),
        out_shape=[shape(4, bf), shape(2, bf), shape(2, bf), shape(2, bf), jax.ShapeDtypeStruct((tokens, depth), bf)],
        grid_spec=pltpu.PrefetchScalarGridSpec(
            num_scalar_prefetch=1,
            grid=(len(out_order),),
            in_specs=[pl.BlockSpec(v.shape, whole) for v in (x, gain, is_hidden, scales)] + columns,
            out_specs=[block(0, 4), block(4, 2), block(6, 2), block(8, 2), pl.BlockSpec((tokens, depth), whole)],
        ),
        compiler_params=params,
        cost_estimate=cost(len(out_order)),
        name="mix_sent",
    )(jnp.stack(out_order), x, gain, is_hidden, scales, *pieces)
    a_keep, b_keep = pl.pallas_call(
        functools.partial(keep_kernel, len(pieces)),
        out_shape=[shape(4, f32), shape(2, f32)],
        grid_spec=pltpu.PrefetchScalarGridSpec(
            num_scalar_prefetch=1,
            grid=(len(own_order),),
            in_specs=[pl.BlockSpec((tokens, depth), whole)] + columns,
            out_specs=[block(0, 4), block(4, 2)],
        ),
        compiler_params=params,
        cost_estimate=cost(len(own_order)),
        name="mix_kept",
    )(jnp.stack(own_order), left, *pieces)
    return a_send, a_keep, b_1, b_2, b_3, b_keep


def fold_kernel(a_keep, a_in, b_keep, b_1, b_2, b_3, a_1, a_2, a_3, a_own, b_send, b_own):
    for i, ref in enumerate((a_1, a_2, a_3, a_own)):
        ref[...] = (a_keep[i] + a_in[i].astype(f32)).astype(ref.dtype)
    for i, ref in enumerate((b_send, b_own)):
        total = b_keep[i] + b_1[i].astype(f32) + b_2[i].astype(f32) + b_3[i].astype(f32)
        ref[...] = total.astype(ref.dtype)


def last_kernel(a_own, a_1, a_2, a_3, b_own, b_in, out_ref):
    half = a_own.shape[1]
    out_ref[:, :half] = (a_own[...] + a_1[...].astype(f32) + a_2[...].astype(f32) + a_3[...].astype(f32)).astype(bf)
    out_ref[:, half:] = (b_own[...] + b_in[...].astype(f32)).astype(bf)


def fold(a_send, a_keep, b_1, b_2, b_3, b_keep, step=128):
    count = lax.axis_size("section")
    _, tokens, half = a_keep.shape

    def to(a, dz, dy):
        pairs = [(i, ((i // 4 + dz) % 2) * 4 + (i % 4 + dy) % 4) for i in range(count)]
        return lax.ppermute(a, "section", pairs)

    b_in = [to(b, 0, d) for b, d in ((b_1, 1), (b_2, 2), (b_3, 3))]
    a_in = to(a_send, 1, 0)
    deep = lambda n: pl.BlockSpec((n, step, half), lambda i: (0, i, 0))
    flat = pl.BlockSpec((step, half), lambda i: (i, 0))
    shape = lambda kind: jax.ShapeDtypeStruct((tokens, half), kind)
    a_1, a_2, a_3, a_own, b_send, b_own = pl.pallas_call(
        fold_kernel,
        out_shape=[shape(bf)] * 3 + [shape(f32), shape(bf), shape(f32)],
        grid=(tokens // step,),
        in_specs=[deep(4), deep(4), deep(2), deep(2), deep(2), deep(2)],
        out_specs=[flat] * 6,
        compiler_params=pltpu.CompilerParams(vmem_limit_bytes=58 << 20),
        name="fold",
    )(a_keep, a_in, b_keep, *b_in)
    a_more = [to(a, 0, d) for a, d in ((a_1, 1), (a_2, 2), (a_3, 3))]
    b_more = to(b_send, 1, 0)
    return pl.pallas_call(
        last_kernel,
        out_shape=jax.ShapeDtypeStruct((tokens, 2 * half), bf),
        grid=(tokens // step,),
        in_specs=[flat] * 6,
        out_specs=pl.BlockSpec((step, 2 * half), lambda i: (i, 0)),
        compiler_params=pltpu.CompilerParams(vmem_limit_bytes=16 << 20),
        name="last",
    )(a_own, *a_more, b_own, b_more)


def spread(w):
    f = lax.axis_index("fsdp")
    z, x, c = f // 8, (f // 2) % 4, f % 2

    def to(a, dz, dx, dc=0):
        pairs = []
        for i in range(lax.axis_size("fsdp")):
            iz, ix, ic = i // 8, (i // 2) % 4, i % 2
            pairs.append((i, ((iz + dz) % 4) * 8 + ((ix + dx) % 4) * 2 + (ic ^ dc)))
        return lax.ppermute(a, "fsdp", pairs)

    line = jnp.concatenate([w, to(w, 1, 0), to(w, -1, 0), to(w, 2, 0)], axis=0)
    own = jnp.concatenate([line, to(line, 0, 1), to(line, 0, -1), to(line, 0, 2)], axis=0)
    pieces = [own, to(own, 0, 0, 1)]
    home = [
        ((z + dz) % 4) * 8 + ((x + dx) % 4) * 2 + (c ^ dc)
        for dc in range(2)
        for dx in (0, -1, 1, 2)
        for dz in (0, -1, 1, 2)
    ]
    return line, pieces, jnp.stack(home)


HEAD = 40


def on_device(hidden, token_ids, table, gain_hidden, gain_embed, proj_hidden, proj_embed):
    width = gain_hidden.shape[0]
    tokens, block = hidden.shape
    rows, out_width = proj_hidden.shape
    sections = lax.axis_size("section")
    groups = lax.axis_size("fsdp")
    section = lax.axis_index("section")
    both = jnp.concatenate([proj_hidden, proj_embed], axis=0)
    depth = 2 * rows

    ids = lax.all_to_all(
        jnp.broadcast_to(token_ids[None], (groups, tokens)), "fsdp", split_axis=0, concat_axis=0, tiled=True
    )
    main = lax.all_gather(both[:HEAD], "fsdp", axis=0, tiled=True)

    turned = turn(table)
    ids = jnp.roll(ids.reshape(-1), -1).reshape(groups, tokens)
    looked = look(turned, ids)
    tail_rows = both[HEAD:]
    e = lax.all_to_all(looked, "fsdp", split_axis=0, concat_axis=0, tiled=True)
    line, pieces, home = spread(tail_rows)

    f, r = jnp.arange(groups)[:, None], jnp.arange(depth)[None, :]

    def place(f, r):
        return jnp.where(r < rows, groups * PAD + f * rows + r, f * PAD + r - rows).reshape(-1)

    source = jnp.concatenate([place(f, r[:, :HEAD]), place(home[:, None], r[:, HEAD:])])[None, :]
    is_hidden = (source >= groups * PAD).astype(f32)
    gain_h = lax.dynamic_slice_in_dim(gain_hidden, section * block, block).reshape(groups, rows)
    gain_e = lax.dynamic_slice_in_dim(gain_embed, section * block, block).reshape(groups, rows)
    gains = jnp.concatenate([gain_h, gain_e], axis=1)
    gain_t = jnp.sum(jnp.where(home[:, None, None] == f[None], gains[None, :, HEAD:], 0.0), axis=1)
    gain = jnp.concatenate([gains[:, :HEAD].reshape(-1), gain_t.reshape(-1)])[None, :]
    hf = hidden.astype(f32)
    ef = e.astype(f32)
    squares = jnp.stack([jnp.sum(hf * hf, axis=1), jnp.sum(ef * ef, axis=(0, 1))])
    squares = lax.all_to_all(
        jnp.broadcast_to(squares[None], (sections, 2, tokens)), "section", split_axis=0, concat_axis=0, tiled=True
    )
    scales = lax.rsqrt(jnp.sum(squares, axis=0) / width + EPS)
    x = prep(hidden, e, source)
    return fold(*mix(x, gain, is_hidden, scales, [main] + pieces, sections))


def solution(mesh):
    placed = (
        P("fsdp", "section"),
        P("fsdp"),
        P(("section", "fsdp"), None),
        P(),
        P(),
        P(("section", "fsdp"), None),
        P(("section", "fsdp"), None),
    )
    return jax.shard_map(
        on_device, mesh=mesh, in_specs=placed, out_specs=P("fsdp", "section"), check_vma=False
    )
```
